32 devices in a mesh: turb: 16 (over z, x, core), snap: 2 (over y).
Axes of the slice: x: 2, y: 2, z: 4, core: 2. Of those that a mesh axis runs over, the one named last changes fastest.
Arguments:
- velocity: bfloat16 [128, 2, 128, 128], P('turb', 'snap'), may hold values from -6 to 6
- turbine_rows: int32 [128], replicated, may hold values from 0 to 127, as said below
- wake_pairs: int32 [256, 2], P('turb'), may hold values from 0 to 127, as said below
Outputs:
- pair_corr: float32 [256, 128, 128], P('turb', 'snap')
- turbine_corr: float32 [128, 2, 128, 128], P('turb', None, 'snap')
The draws below stay inside these ranges and needn't reach their ends.
Inputs may be any that keep to these rules, and one draw needn't show every extreme that they name: `turbine_rows`: A permutation of the turbines. `wake_pairs`: the 16 pairs of each aligned block of 16 rows (those of one turbine group) name 32 different turbines. Of these, at most 2 have storage rows of any one group (rows g * 8 to (g + 1) * 8 - 1), and in every block some group has exactly 2.
All inputs are finite; a program needn't handle non-finite values.
Results may differ from the reference program's by a relative error of at most 0.0089.
Values may be sent and summed in bfloat16 or wider, within the bound.
A program may use at most 64 MiB of HBM per device.

```python
import jax
import jax.numpy as jnp
from jax import lax

P_SIZE = 128
TURB_DEV = 8
TURBINES = 128
SNAPS = 2
PAIR_DEV = 16
PAIRS = 256
CAP = 2
N_TURB = 16


def wake_layout(key):
    group_count = TURBINES // TURB_DEV
    cell_count = group_count * CAP
    turbine_home = jax.random.permutation(jax.random.fold_in(key, 101), TURBINES).astype(jnp.int32)
    inverse = jnp.argsort(turbine_home).astype(jnp.int32)
    popularity = jax.random.randint(jax.random.fold_in(key, 102), (group_count,), 0, 4).astype(jnp.int32)
    source = jnp.broadcast_to(jnp.arange(group_count, dtype=jnp.int32)[:, None], (group_count, CAP))
    cell_ids = jnp.arange(cell_count, dtype=jnp.int32).reshape(group_count, CAP)
    pair_ends = 2 * PAIR_DEV

    def one_group(group_index):
        group_key = jax.random.fold_in(key, 1000 + group_index)
        noise_bits = jax.random.randint(jax.random.fold_in(group_key, 1), (group_count, CAP), 0, 4096).astype(jnp.int32)
        forced = (source == (group_index + 1) % group_count).astype(jnp.int32)
        scores = ((forced * 4 + popularity[:, None]) * 4096 + noise_bits) * cell_count + (cell_count - 1 - cell_ids)
        chosen = jnp.argsort(-scores.reshape(-1))[:pair_ends]
        pick_bits = jax.random.randint(jax.random.fold_in(group_key, 2), (group_count, TURB_DEV), 0, 65536).astype(jnp.int32)
        pick_bits = pick_bits * TURB_DEV + jnp.arange(TURB_DEV, dtype=jnp.int32)[None, :]
        offsets = jnp.argsort(pick_bits, axis=1)[:, :CAP].astype(jnp.int32)
        row_ids = (source * TURB_DEV + offsets).reshape(-1)[chosen]
        shuffle = jax.random.permutation(jax.random.fold_in(group_key, 3), pair_ends)
        row_ids = row_ids[shuffle]
        return jnp.stack([row_ids[:PAIR_DEV], row_ids[PAIR_DEV:]], axis=1)
    row_ids = jax.vmap(one_group)(jnp.arange(group_count, dtype=jnp.int32)).reshape(-1, 2)
    return (turbine_home, inverse[row_ids].astype(jnp.int32))


def draw_turbine_rows(key, part):
    return wake_layout(key)[0]


def draw_wake_pairs(key, part):
    return wake_layout(key)[1]


def levels(rng, extent, pieces, least, high):
    def one(axis_at, parts):
        steps = jax.random.uniform(jax.random.fold_in(jax.random.fold_in(rng, 6), axis_at), (parts,), jnp.float32, least / len(pieces), high / len(pieces))
        return jnp.repeat(jnp.exp(steps), extent[axis_at] // parts).reshape((-1,) + (1,) * (len(extent) - axis_at - 1))

    level = one(*pieces[0])
    for cut in pieces[1:]:
        level = level * one(*cut)
    return level


def centred(stream_key, extent, spread, reach, split=(), kind=jnp.bfloat16):
    entries = jax.random.normal(stream_key, extent, jnp.float32) * spread
    if len(split) > 0:
        entries = levels(stream_key, extent, split, -0.22, 0.18) * entries
    return jnp.clip(entries, min=-reach, max=reach).astype(kind)


def setup_inputs(seed: int = 0) -> dict:
    splits = jax.random.split(jax.random.key(seed), 4)
    velocity = centred(splits[0], (TURBINES, SNAPS, P_SIZE, P_SIZE), 1.0, 6.0, ((0, 16), (1, 2)))
    turbine_rows = draw_turbine_rows(jax.random.fold_in(splits[3], 71), 0)
    wake_pairs = draw_wake_pairs(jax.random.fold_in(splits[3], 71), 0)
    return {"velocity": velocity, "turbine_rows": turbine_rows, "wake_pairs": wake_pairs}


def basis_tables(side_cells):
    ramp_index = jnp.arange(side_cells, dtype=jnp.int32)
    folded = ramp_index[:, None] * ramp_index[None, :] % side_cells
    angles = folded.astype(jnp.float32) * (2.0 * jnp.pi / side_cells)
    scale_factor = 1.0 / jnp.sqrt(jnp.float32(side_cells))
    return (jnp.cos(angles) * scale_factor, -jnp.sin(angles) * scale_factor)

def forward_planes(planes, narrow_re, narrow_im):
    side_cells = planes.shape[-1]
    highest = lax.Precision.HIGHEST
    flat_rows = planes.reshape(-1, side_cells)
    half_re = jnp.dot(flat_rows, narrow_re, preferred_element_type=jnp.float32).astype(jnp.bfloat16)
    half_im = jnp.dot(flat_rows, narrow_im, preferred_element_type=jnp.float32).astype(jnp.bfloat16)
    half_re = half_re.astype(jnp.float32).reshape(-1, side_cells, side_cells)
    half_im = half_im.astype(jnp.float32).reshape(-1, side_cells, side_cells)
    left_re = narrow_re.astype(jnp.float32)
    left_im = narrow_im.astype(jnp.float32)
    real_part = jnp.einsum('ca,nab->ncb', left_re, half_re, precision=highest) - jnp.einsum('ca,nab->ncb', left_im, half_im, precision=highest)
    imag_part = jnp.einsum('ca,nab->ncb', left_re, half_im, precision=highest) + jnp.einsum('ca,nab->ncb', left_im, half_re, precision=highest)
    return jnp.stack([real_part, imag_part], axis=1).astype(jnp.bfloat16)

def inverse_pairs(cross_spec, wide_re, wide_im):
    highest = lax.Precision.HIGHEST
    cross_re = cross_spec[:, 0]
    cross_im = cross_spec[:, 1]
    mixed_re = jnp.einsum('ca,nab->ncb', wide_re, cross_re, precision=highest) + jnp.einsum('ca,nab->ncb', wide_im, cross_im, precision=highest)
    mixed_im = jnp.einsum('ca,nab->ncb', wide_re, cross_im, precision=highest) - jnp.einsum('ca,nab->ncb', wide_im, cross_re, precision=highest)
    return jnp.einsum('nab,bc->nac', mixed_re, wide_re, precision=highest) + jnp.einsum('nab,bc->nac', mixed_im, wide_im, precision=highest)

def reference(velocity, turbine_rows, wake_pairs):
    wide_re, wide_im = basis_tables(P_SIZE)
    narrow_re = wide_re.astype(jnp.bfloat16)
    narrow_im = wide_im.astype(jnp.bfloat16)
    spectra = lax.map(lambda planes: forward_planes(planes, narrow_re, narrow_im), velocity)
    row_ids = jnp.take(turbine_rows, wake_pairs, axis=0).astype(jnp.int32)
    blocks = row_ids.reshape(N_TURB, PAIR_DEV, 2)

    def one_block(block_rows):
        upstream = jnp.take(spectra, block_rows[:, 0], axis=0).astype(jnp.float32)
        downstream = jnp.take(spectra, block_rows[:, 1], axis=0).astype(jnp.float32)
        cross_re = lax.optimization_barrier(jnp.sum(upstream[:, :, 0] * downstream[:, :, 0] + upstream[:, :, 1] * downstream[:, :, 1], axis=1)) / SNAPS
        cross_im = lax.optimization_barrier(jnp.sum(upstream[:, :, 0] * downstream[:, :, 1] - upstream[:, :, 1] * downstream[:, :, 0], axis=1)) / SNAPS
        return inverse_pairs(jnp.stack([cross_re, cross_im], axis=1), wide_re, wide_im)
    pair_corr = lax.map(one_block, blocks).reshape(PAIRS, P_SIZE, P_SIZE)
    turbine_corr = jnp.zeros((TURBINES, 2, P_SIZE, P_SIZE), jnp.float32)
    turbine_corr = turbine_corr.at[row_ids[:, 0], 0].add(pair_corr)
    turbine_corr = turbine_corr.at[row_ids[:, 1], 1].add(pair_corr)
    return (pair_corr, turbine_corr)
```

```python
import functools

import jax
import jax.numpy as jnp
from jax import lax
from jax.experimental import pallas as pl
from jax.experimental.pallas import tpu as pltpu
from jax.sharding import PartitionSpec as P

MESH = pl.DeviceIdType.MESH
CAP = 2
BATCH = 4


def basis_tables(side):
    ramp = jnp.arange(side, dtype=jnp.int32)
    folded = ramp[:, None] * ramp[None, :] % side
    angles = folded.astype(jnp.float32) * (2.0 * jnp.pi / side)
    scale = 1.0 / jnp.sqrt(jnp.float32(side))
    return (jnp.cos(angles) * scale, -jnp.sin(angles) * scale)


def dot(a, b):
    return jnp.dot(a, b, preferred_element_type=jnp.float32)


def kernel(
    n,
    ns,
    slot_ref,
    owner_ref,
    vel,
    wanted,
    right_fwd,
    left_fwd,
    left_inv,
    right_inv,
    pair_out,
    turb_out,
    req,
    req_s,
    sendb,
    recvb,
    spec,
    part,
    ssend,
    srecv,
    bsend,
    brecv,
    local_sem,
    req_send,
    req_recv,
    fwd_send,
    fwd_recv,
    snap_send,
    snap_recv,
    back_send,
    back_recv,
):
    me = lax.axis_index("turb")
    sn = lax.axis_index("snap")
    side = vel.shape[-1]
    pairs, rows = pair_out.shape[:2]
    outs = 2 * turb_out.shape[0]
    chunks = pairs // BATCH

    def ahead(k):
        return lax.rem(me + k, n)

    def behind(k):
        return lax.rem(me + n - k, n)

    def snap_at(j):
        return lax.rem(sn + j, ns)

    def loop(lo, hi, step):
        def wrapped(i, carry):
            step(i)
            return carry

        lax.fori_loop(lo, hi, wrapped, 0)

    barrier = pltpu.get_barrier_semaphore()
    loop(1, n, lambda k: pl.semaphore_signal(barrier, inc=1, device_id={"turb": ahead(k)}, device_id_type=MESH))
    loop(1, ns, lambda j: pl.semaphore_signal(barrier, inc=1, device_id={"snap": snap_at(j)}, device_id_type=MESH))
    pl.semaphore_wait(barrier, n + ns - 2)

    def req_copy(k):
        return pltpu.make_async_remote_copy(
            wanted.at[k], req.at[k], req_send.at[k], req_recv.at[k],
            device_id={"turb": behind(k)}, device_id_type=MESH,
        )

    def fwd_copy(k):
        return pltpu.make_async_remote_copy(
            sendb.at[k], recvb.at[k], fwd_send.at[k], fwd_recv.at[k],
            device_id={"turb": ahead(k)}, device_id_type=MESH,
        )

    def snap_copy(j, c):
        span = pl.ds(c * BATCH, BATCH)
        return pltpu.make_async_remote_copy(
            ssend.at[j, span], srecv.at[j, span], snap_send.at[j, c], snap_recv.at[j, c],
            device_id={"snap": snap_at(j)}, device_id_type=MESH,
        )

    def back_copy(k):
        return pltpu.make_async_remote_copy(
            bsend.at[k], brecv.at[k], back_send.at[k], back_recv.at[k],
            device_id={"turb": behind(k)}, device_id_type=MESH,
        )

    loop(1, n, lambda k: req_copy(k).start())
    req[0] = wanted[0]
    loop(1, n, lambda k: req_copy(k).wait_recv())
    to_scalars = pltpu.make_async_copy(req, req_s, local_sem)
    to_scalars.start()
    to_scalars.wait()

    def send_planes(k):
        for c in range(CAP):
            sendb[k, c] = vel[req_s[k, 0, CAP + c]]
        fwd_copy(k).start()

    loop(1, n, send_planes)
    for c in range(CAP):
        recvb[0, c] = vel[req_s[0, 0, CAP + c]]

    def forward(k):
        planes = recvb[k].reshape(CAP * side, side)
        half = dot(planes, right_fwd[...]).astype(jnp.bfloat16)
        top = jnp.concatenate([half[:side, :side], half[side:, :side]], axis=1)
        low = jnp.concatenate([half[:side, side:], half[side:, side:]], axis=1)
        both = dot(left_fwd[...], jnp.concatenate([top, low], axis=0)).astype(jnp.bfloat16)
        spec[k * CAP] = both[:, :side]
        spec[k * CAP + 1] = both[:, side:]

    forward(0)

    def arrive(k):
        fwd_copy(k).wait_recv()
        forward(k)

    loop(1, n, arrive)

    def cross(p):
        up = spec[slot_ref[p]].astype(jnp.float32)
        down = spec[slot_ref[pairs + p]].astype(jnp.float32)
        ur, ui, dr, di = up[:side], up[side:], down[:side], down[side:]
        both = jnp.concatenate([ur * dr + ui * di, ur * di - ui * dr], axis=0)
        return (both * (1.0 / ns)).astype(jnp.bfloat16)

    def pair_chunk(c):
        for b in range(0, BATCH, 2):
            p = c * BATCH + b
            mixed = dot(left_inv[...], jnp.concatenate([cross(p), cross(p + 1)], axis=1)).astype(jnp.bfloat16)
            wide = jnp.concatenate(
                [
                    jnp.concatenate([mixed[:side, :side], mixed[side:, :side]], axis=1),
                    jnp.concatenate([mixed[:side, side:], mixed[side:, side:]], axis=1),
                ],
                axis=0,
            )
            out = dot(wide, right_inv[...])
            part[b] = out[:side]
            part[b + 1] = out[side:]
        for b in range(BATCH):
            p = c * BATCH + b
            pair_out[p] = part[b, pl.ds(pl.multiple_of(sn * rows, rows), rows)]

            def give(j):
                at = pl.multiple_of(snap_at(j) * rows, rows)
                ssend[j, p] = part[b, pl.ds(at, rows)].astype(jnp.bfloat16)

            loop(1, ns, give)
        loop(1, ns, lambda j: snap_copy(j, c).start())

    loop(0, chunks, pair_chunk)

    def collect(c):
        def one(j):
            snap_copy(j, c).wait_recv()
            for b in range(BATCH):
                p = c * BATCH + b
                pair_out[p] = pair_out[p] + srecv[j, p].astype(jnp.float32)

        loop(1, ns, one)

    loop(0, chunks, collect)

    def send_back(k):
        for c in range(CAP):
            bsend[k, c] = pair_out[owner_ref[k * CAP + c]].astype(jnp.bfloat16)
        back_copy(k).start()

    loop(1, n, send_back)
    for c in range(CAP):
        brecv[0, c] = pair_out[owner_ref[c]].astype(jnp.bfloat16)

    turb_out[...] = jnp.zeros_like(turb_out)

    def total(k):
        got = [brecv[k, c].astype(jnp.float32) for c in range(CAP)]
        codes = [req_s[k, 0, c] for c in range(CAP)]
        for o in range(outs):
            add = turb_out[o // 2, o % 2]
            for c in range(CAP):
                add = add + got[c] * jnp.where(codes[c] == o, 1.0, 0.0)
            turb_out[o // 2, o % 2] = add

    total(0)

    def returned(k):
        back_copy(k).wait_recv()
        total(k)

    loop(1, n, returned)

    def drain(k):
        req_copy(k).wait_send()
        fwd_copy(k).wait_send()
        back_copy(k).wait_send()

    loop(1, n, drain)
    loop(0, chunks, lambda c: loop(1, ns, lambda j: snap_copy(j, c).wait_send()))


def body(velocity, turbine_rows, wake_pairs):
    n = lax.axis_size("turb")
    ns = lax.axis_size("snap")
    me = lax.axis_index("turb")
    local_turb, local_snaps, side = velocity.shape[:3]
    assert local_snaps == 1
    pairs = wake_pairs.shape[0]
    slots = n * CAP
    rows = side // ns
    wide_re, wide_im = basis_tables(side)
    re, im = wide_re.astype(jnp.bfloat16), wide_im.astype(jnp.bfloat16)
    right_fwd = jnp.concatenate([re, im], axis=1)
    left_fwd = jnp.concatenate([jnp.concatenate([re, -im], 1), jnp.concatenate([im, re], 1)], 0)
    left_inv = jnp.concatenate([jnp.concatenate([re, im], 1), jnp.concatenate([-im, re], 1)], 0)
    right_inv = jnp.concatenate([re, im], axis=0)

    ends = wake_pairs.T.reshape(-1)
    turbines = jnp.arange(turbine_rows.shape[0], dtype=jnp.int32)
    end_rows = jnp.sum(jnp.where(ends[:, None] == turbines[None, :], turbine_rows[None, :], 0), axis=1)
    end_index = jnp.arange(2 * pairs, dtype=jnp.int32)
    group = end_rows // local_turb
    same = (group[:, None] == group[None, :]) & (end_index[None, :] < end_index[:, None])
    rank = jnp.sum(same.astype(jnp.int32), axis=1)
    slot = lax.rem(me + n - group, n) * CAP + rank
    code = end_rows % local_turb * 2 + (end_index >= pairs).astype(jnp.int32)
    hits = slot[None, :] == jnp.arange(slots, dtype=jnp.int32)[:, None]
    codes = jnp.sum(jnp.where(hits, code[None, :] + 1, 0), axis=1) - 1
    owner = jnp.sum(jnp.where(hits, end_index[None, :] % pairs, 0), axis=1)
    codes = codes.reshape(n, CAP)
    wanted = jnp.concatenate([codes, jnp.maximum(codes, 0) // 2], axis=1)
    wanted = jnp.pad(wanted, ((0, 0), (0, 128 - 2 * CAP)))[:, None, :]

    vmem = pl.BlockSpec(memory_space=pltpu.VMEM)
    smem = pl.BlockSpec(memory_space=pltpu.SMEM)
    chunks = pairs // BATCH
    bf16 = jnp.bfloat16
    sem = pltpu.SemaphoreType.DMA
    return pl.pallas_call(
        functools.partial(kernel, n, ns),
        out_shape=(
            jax.ShapeDtypeStruct((pairs, rows, side), jnp.float32),
            jax.ShapeDtypeStruct((local_turb, 2, rows, side), jnp.float32),
        ),
        in_specs=[smem, smem] + [vmem] * 6,
        out_specs=(vmem, vmem),
        scratch_shapes=[
            pltpu.VMEM((n, 1, 128), jnp.int32),
            pltpu.SMEM((n, 1, 128), jnp.int32),
            pltpu.VMEM((n, CAP, side, side), bf16),
            pltpu.VMEM((n, CAP, side, side), bf16),
            pltpu.VMEM((slots, 2 * side, side), bf16),
            pltpu.VMEM((BATCH, side, side), jnp.float32),
            pltpu.VMEM((ns, pairs, rows, side), bf16),
            pltpu.VMEM((ns, pairs, rows, side), bf16),
            pltpu.VMEM((n, CAP, rows, side), bf16),
            pltpu.VMEM((n, CAP, rows, side), bf16),
            sem,
            sem((n,)),
            sem((n,)),
            sem((n,)),
            sem((n,)),
            sem((ns, chunks)),
            sem((ns, chunks)),
            sem((n,)),
            sem((n,)),
        ],
        compiler_params=pltpu.CompilerParams(
            collective_id=0, has_side_effects=True, vmem_limit_bytes=48 * 2**20
        ),
    )(slot, owner, velocity[:, 0], wanted, right_fwd, left_fwd, left_inv, right_inv)


def solution(mesh):
    return jax.shard_map(
        body,
        mesh=mesh,
        in_specs=(P("turb", "snap", None, None), P(), P("turb", None)),
        out_specs=(P("turb", "snap", None), P("turb", None, "snap", None)),
        check_vma=False,
    )
```

```python
import functools

import jax
import jax.numpy as jnp
import ml_dtypes
import numpy as np
from jax import lax
from jax.experimental import pallas as pl
from jax.experimental.pallas import tpu as pltpu
from jax.sharding import PartitionSpec as P

MESH = pl.DeviceIdType.MESH
CAP = 2
BATCH = 4
CUTS = 4


def basis_tables(side):
    ramp = np.arange(side, dtype=np.int32)
    angles = (ramp[:, None] * ramp[None, :] % side) * (2.0 * np.pi / side)
    return (
        (np.cos(angles) / np.sqrt(side)).astype(np.float32),
        (-np.sin(angles) / np.sqrt(side)).astype(np.float32),
    )


def dot(a, b):
    return jnp.dot(a, b, preferred_element_type=jnp.float32)


def tables(n, me, local_turb, turb_rows, wake):
    pairs = wake.shape[0]
    count = 2 * pairs
    shift = local_turb.bit_length() - 1
    total = turb_rows.shape[1]
    ends = jnp.concatenate([wake[:, 0:1], wake[:, 1:2]], axis=0)
    lanes = lax.broadcasted_iota(jnp.int32, (count, total), 1)
    rows_col = jnp.sum(jnp.where(ends == lanes, turb_rows[...], 0), axis=1, keepdims=True)
    down = lax.broadcasted_iota(jnp.int32, (count, count), 0)
    over = lax.broadcasted_iota(jnp.int32, (count, count), 1)
    rows_row = jnp.sum(jnp.where(down == over, rows_col, 0), axis=0, keepdims=True)
    group_col = lax.shift_right_logical(rows_col, jnp.full_like(rows_col, shift))
    group_row = lax.shift_right_logical(rows_row, jnp.full_like(rows_row, shift))
    same = (group_col == group_row) & (down < over)
    rank = jnp.sum(jnp.where(same, 1, 0), axis=0, keepdims=True)
    back = me - group_row
    slot = jnp.where(back < 0, back + n, back) * CAP + rank
    end = lax.broadcasted_iota(jnp.int32, (1, count), 1)
    code = (rows_row - group_row * local_turb) * 2 + jnp.where(end >= pairs, 1, 0)
    pair = jnp.where(end >= pairs, end - pairs, end)
    place = lax.broadcasted_iota(jnp.int32, (n, count), 0)
    lane = lax.broadcasted_iota(jnp.int32, (n, 128), 1)
    table = jnp.zeros((n, 128), jnp.int32)
    for c in range(CAP):
        hit = slot == place * CAP + c
        codes = jnp.sum(jnp.where(hit, code + 1, 0), axis=1, keepdims=True) - 1
        owner = jnp.sum(jnp.where(hit, pair, 0), axis=1, keepdims=True)
        plane = lax.shift_right_logical(jnp.maximum(codes, 0), jnp.ones_like(codes))
        table = jnp.where(lane == c, codes, table)
        table = jnp.where(lane == CAP + c, plane, table)
        table = jnp.where(lane == 2 * CAP + c, owner, table)
    last = jnp.concatenate([jnp.minimum(slot, n * CAP - 1), jnp.zeros((1, 128 - count), jnp.int32)], axis=1)
    return jnp.concatenate([table, last], axis=0)


def kernel(
    n,
    ns,
    vel_hbm,
    turb_rows,
    wake,
    right_fwd_hbm,
    left_fwd_hbm,
    left_inv_hbm,
    right_inv_hbm,
    pair_out,
    turb_out,
    vel,
    right_fwd,
    left_fwd,
    left_inv,
    right_inv,
    wanted,
    own_s,
    req,
    req_s,
    sendb,
    recvb,
    spec,
    part,
    ssend,
    srecv,
    bsend,
    brecv,
    load_sem,
    own_sem,
    local_sem,
    req_send,
    req_recv,
    fwd_send,
    fwd_recv,
    snap_send,
    snap_recv,
    back_send,
    back_recv,
):
    me = lax.axis_index("turb")
    sn = lax.axis_index("snap")
    side = vel.shape[-1]
    pairs, rows = pair_out.shape[:2]
    outs = 2 * turb_out.shape[0]
    chunks = pairs // BATCH
    cuts, tall = bsend.shape[1], bsend.shape[3]

    def ahead(k):
        return lax.rem(me + k, n)

    def behind(k):
        return lax.rem(me + n - k, n)

    def snap_at(j):
        return lax.rem(sn + j, ns)

    def loop(lo, hi, step):
        def wrapped(i, carry):
            step(i)
            return carry

        lax.fori_loop(lo, hi, wrapped, 0)

    loads = [
        pltpu.make_async_copy(a, b, load_sem.at[i])
        for i, (a, b) in enumerate(
            [
                (vel_hbm, vel),
                (right_fwd_hbm, right_fwd),
                (left_fwd_hbm, left_fwd),
                (left_inv_hbm, left_inv),
                (right_inv_hbm, right_inv),
            ]
        )
    ]
    barrier = pltpu.get_barrier_semaphore()
    loop(1, n, lambda k: pl.semaphore_signal(barrier, inc=1, device_id={"turb": ahead(k)}, device_id_type=MESH))
    loop(1, ns, lambda j: pl.semaphore_signal(barrier, inc=1, device_id={"snap": snap_at(j)}, device_id_type=MESH))
    for load in loads:
        load.start()
    wanted[...] = tables(n, me, turb_out.shape[0], turb_rows, wake)[:, None, :]
    own = pltpu.make_async_copy(wanted, own_s, own_sem)
    own.start()
    pl.semaphore_wait(barrier, n + ns - 2)

    def req_copy(k):
        return pltpu.make_async_remote_copy(
            wanted.at[k], req.at[k], req_send.at[k], req_recv.at[k],
            device_id={"turb": behind(k)}, device_id_type=MESH,
        )

    def fwd_copy(k):
        return pltpu.make_async_remote_copy(
            sendb.at[k], recvb.at[k], fwd_send.at[k], fwd_recv.at[k],
            device_id={"turb": ahead(k)}, device_id_type=MESH,
        )

    def snap_copy(j, r):
        return pltpu.make_async_remote_copy(
            ssend.at[j, r], srecv.at[j, r], snap_send.at[j, r], snap_recv.at[j, r],
            device_id={"snap": snap_at(j)}, device_id_type=MESH,
        )

    def back_copy(k, r):
        return pltpu.make_async_remote_copy(
            bsend.at[k, r], brecv.at[k, r], back_send.at[k, r], back_recv.at[k, r],
            device_id={"turb": behind(k)}, device_id_type=MESH,
        )

    loop(1, n, lambda k: req_copy(k).start())
    req[0] = wanted[0]
    loop(1, n, lambda k: req_copy(k).wait_recv())
    to_scalars = pltpu.make_async_copy(req, req_s, local_sem)
    to_scalars.start()
    to_scalars.wait()
    own.wait()
    for load in loads:
        load.wait()

    def send_planes(k):
        for c in range(CAP):
            sendb[k, c] = vel[req_s[k, 0, CAP + c]]
        fwd_copy(k).start()

    loop(1, n, send_planes)
    for c in range(CAP):
        recvb[0, c] = vel[req_s[0, 0, CAP + c]]

    def forward(k):
        planes = recvb[k].reshape(CAP * side, side)
        half = dot(planes, right_fwd[...]).astype(jnp.bfloat16)
        top = jnp.concatenate([half[:side, :side], half[side:, :side]], axis=1)
        low = jnp.concatenate([half[:side, side:], half[side:, side:]], axis=1)
        both = dot(left_fwd[...], jnp.concatenate([top, low], axis=0)).astype(jnp.bfloat16)
        spec[k * CAP] = both[:, :side]
        spec[k * CAP + 1] = both[:, side:]

    forward(0)

    def arrive(k):
        fwd_copy(k).wait_recv()
        forward(k)

    loop(1, n, arrive)

    def cross(p):
        up = spec[own_s[n, 0, p]].astype(jnp.float32)
        down = spec[own_s[n, 0, pairs + p]].astype(jnp.float32)
        ur, ui, dr, di = up[:side], up[side:], down[:side], down[side:]
        both = jnp.concatenate([ur * dr + ui * di, ur * di - ui * dr], axis=0)
        return (both * (1.0 / ns)).astype(jnp.bfloat16)

    def pair_chunk(c):
        for b in range(0, BATCH, 2):
            p = c * BATCH + b
            mixed = dot(left_inv[...], jnp.concatenate([cross(p), cross(p + 1)], axis=1)).astype(jnp.bfloat16)
            wide = jnp.concatenate(
                [
                    jnp.concatenate([mixed[:side, :side], mixed[side:, :side]], axis=1),
                    jnp.concatenate([mixed[:side, side:], mixed[side:, side:]], axis=1),
                ],
                axis=0,
            )
            out = dot(wide, right_inv[...])
            part[b] = out[:side]
            part[b + 1] = out[side:]
        for b in range(BATCH):
            p = c * BATCH + b
            pair_out[p] = part[b, pl.ds(pl.multiple_of(sn * rows, rows), rows)]

            def give(j):
                for r in range(cuts):
                    at = pl.multiple_of(snap_at(j) * rows, rows) + r * tall
                    ssend[j, r, p] = part[b, pl.ds(at, tall)].astype(jnp.bfloat16)

            loop(1, ns, give)

    loop(0, chunks, pair_chunk)
    for r in range(cuts):
        loop(1, ns, lambda j: snap_copy(j, r).start())

    for r in range(cuts):
        span = pl.ds(r * tall, tall)

        def collect(j):
            snap_copy(j, r).wait_recv()
            pair_out[:, span] = pair_out[:, span] + srecv[j, r].astype(jnp.float32)

        loop(1, ns, collect)

        def send_back(k):
            for c in range(CAP):
                bsend[k, r, c] = pair_out[own_s[k, 0, 2 * CAP + c], span].astype(jnp.bfloat16)
            back_copy(k, r).start()

        loop(1, n, send_back)
        for c in range(CAP):
            brecv[0, r, c] = pair_out[own_s[0, 0, 2 * CAP + c], span].astype(jnp.bfloat16)

    turb_out[...] = jnp.zeros_like(turb_out)
    for r in range(cuts):
        span = pl.ds(r * tall, tall)

        def total(k):
            got = [brecv[k, r, c].astype(jnp.float32) for c in range(CAP)]
            codes = [req_s[k, 0, c] for c in range(CAP)]
            for o in range(outs):
                add = turb_out[o // 2, o % 2, span]
                for c in range(CAP):
                    add = add + got[c] * jnp.where(codes[c] == o, 1.0, 0.0)
                turb_out[o // 2, o % 2, span] = add

        total(0)

        def returned(k):
            back_copy(k, r).wait_recv()
            total(k)

        loop(1, n, returned)

    def drain(k):
        req_copy(k).wait_send()
        fwd_copy(k).wait_send()
        for r in range(cuts):
            back_copy(k, r).wait_send()

    loop(1, n, drain)
    for r in range(cuts):
        loop(1, ns, lambda j: snap_copy(j, r).wait_send())


def body(velocity, turbine_rows, wake_pairs):
    n = lax.axis_size("turb")
    ns = lax.axis_size("snap")
    local_turb, local_snaps, side = velocity.shape[:3]
    assert local_snaps == 1
    pairs = wake_pairs.shape[0]
    slots = n * CAP
    rows = side // ns
    cuts = max(1, min(CUTS, rows // 16))
    assert local_turb & (local_turb - 1) == 0 and 2 * pairs <= 128
    wide_re, wide_im = basis_tables(side)
    re, im = wide_re.astype(ml_dtypes.bfloat16), wide_im.astype(ml_dtypes.bfloat16)
    right_fwd = np.concatenate([re, im], axis=1)
    left_fwd = np.block([[re, -im], [im, re]])
    left_inv = np.block([[re, im], [-im, re]])
    right_inv = np.concatenate([re, im], axis=0)
    basis = [jnp.asarray(a) for a in (right_fwd, left_fwd, left_inv, right_inv)]

    vmem = pl.BlockSpec(memory_space=pltpu.VMEM)
    hbm = pl.BlockSpec(memory_space=pl.ANY)
    bf16 = jnp.bfloat16
    sem = pltpu.SemaphoreType.DMA
    return pl.pallas_call(
        functools.partial(kernel, n, ns),
        out_shape=(
            jax.ShapeDtypeStruct((pairs, rows, side), jnp.float32),
            jax.ShapeDtypeStruct((local_turb, 2, rows, side), jnp.float32),
        ),
        in_specs=[hbm, vmem, vmem] + [hbm] * 4,
        out_specs=(vmem, vmem),
        scratch_shapes=[
            pltpu.VMEM((local_turb, side, side), bf16),
            *[pltpu.VMEM(a.shape, bf16) for a in basis],
            pltpu.VMEM((n + 1, 1, 128), jnp.int32),
            pltpu.SMEM((n + 1, 1, 128), jnp.int32),
            pltpu.VMEM((n, 1, 128), jnp.int32),
            pltpu.SMEM((n, 1, 128), jnp.int32),
            pltpu.VMEM((n, CAP, side, side), bf16),
            pltpu.VMEM((n, CAP, side, side), bf16),
            pltpu.VMEM((slots, 2 * side, side), bf16),
            pltpu.VMEM((BATCH, side, side), jnp.float32),
            pltpu.VMEM((ns, cuts, pairs, rows // cuts, side), bf16),
            pltpu.VMEM((ns, cuts, pairs, rows // cuts, side), bf16),
            pltpu.VMEM((n, cuts, CAP, rows // cuts, side), bf16),
            pltpu.VMEM((n, cuts, CAP, rows // cuts, side), bf16),
            sem((5,)),
            sem,
            sem,
            sem((n,)),
            sem((n,)),
            sem((n,)),
            sem((n,)),
            sem((ns, cuts)),
            sem((ns, cuts)),
            sem((n, cuts)),
            sem((n, cuts)),
        ],
        compiler_params=pltpu.CompilerParams(
            collective_id=0, has_side_effects=True, vmem_limit_bytes=48 * 2**20
        ),
    )(velocity[:, 0], turbine_rows[None, :], wake_pairs, *basis)


def solution(mesh):
    return jax.shard_map(
        body,
        mesh=mesh,
        in_specs=(P("turb", "snap", None, None), P(), P("turb", None)),
        out_specs=(P("turb", "snap", None), P("turb", None, "snap", None)),
        check_vma=False,
    )
```

```python
import functools

import jax
import jax.numpy as jnp
import ml_dtypes
import numpy as np
from jax import lax
from jax.experimental import pallas as pl
from jax.experimental.pallas import tpu as pltpu
from jax.sharding import PartitionSpec as P

MESH = pl.DeviceIdType.MESH
CAP = 2
BATCH = 4
CUTS = 2


def basis_tables(side):
    ramp = np.arange(side, dtype=np.int32)
    angles = (ramp[:, None] * ramp[None, :] % side) * (2.0 * np.pi / side)
    return (
        (np.cos(angles) / np.sqrt(side)).astype(np.float32),
        (-np.sin(angles) / np.sqrt(side)).astype(np.float32),
    )


def dot(a, b):
    return jnp.dot(a, b, preferred_element_type=jnp.float32)


def tables(n, me, local_turb, turb_rows, wake):
    pairs = wake.shape[1]
    count = 2 * pairs
    shift = local_turb.bit_length() - 1
    total = turb_rows.shape[1]
    first = lax.broadcasted_iota(jnp.int32, (pairs, pairs), 0)
    second = lax.broadcasted_iota(jnp.int32, (pairs, pairs), 1)
    ends = jnp.concatenate(
        [jnp.sum(jnp.where(first == second, wake[i : i + 1], 0), axis=1, keepdims=True) for i in range(2)], axis=0
    )
    lanes = lax.broadcasted_iota(jnp.int32, (count, total), 1)
    rows_col = jnp.sum(jnp.where(ends == lanes, turb_rows[...], 0), axis=1, keepdims=True)
    down = lax.broadcasted_iota(jnp.int32, (count, count), 0)
    over = lax.broadcasted_iota(jnp.int32, (count, count), 1)
    rows_row = jnp.sum(jnp.where(down == over, rows_col, 0), axis=0, keepdims=True)
    group_col = lax.shift_right_logical(rows_col, jnp.full_like(rows_col, shift))
    group_row = lax.shift_right_logical(rows_row, jnp.full_like(rows_row, shift))
    same = (group_col == group_row) & (down < over)
    rank = jnp.sum(jnp.where(same, 1, 0), axis=0, keepdims=True)
    back = me - group_row
    slot = jnp.where(back < 0, back + n, back) * CAP + rank
    end = lax.broadcasted_iota(jnp.int32, (1, count), 1)
    code = (rows_row - group_row * local_turb) * 2 + jnp.where(end >= pairs, 1, 0)
    pair = jnp.where(end >= pairs, end - pairs, end)
    place = lax.broadcasted_iota(jnp.int32, (n, count), 0)
    lane = lax.broadcasted_iota(jnp.int32, (n, 128), 1)
    table = jnp.zeros((n, 128), jnp.int32)
    for c in range(CAP):
        hit = slot == place * CAP + c
        codes = jnp.sum(jnp.where(hit, code + 1, 0), axis=1, keepdims=True) - 1
        owner = jnp.sum(jnp.where(hit, pair, 0), axis=1, keepdims=True)
        plane = lax.shift_right_logical(jnp.maximum(codes, 0), jnp.ones_like(codes))
        table = jnp.where(lane == c, codes, table)
        table = jnp.where(lane == CAP + c, plane, table)
        table = jnp.where(lane == 2 * CAP + c, owner, table)
    last = jnp.concatenate([jnp.minimum(slot, n * CAP - 1), jnp.zeros((1, 128 - count), jnp.int32)], axis=1)
    return jnp.concatenate([table, last], axis=0)


def kernel(
    n,
    ns,
    vel_hbm,
    turb_rows_hbm,
    wake_hbm,
    right_fwd_hbm,
    left_fwd_hbm,
    left_inv_hbm,
    right_inv_hbm,
    pair_out,
    turb_out,
    turb_rows,
    wake,
    vel,
    right_fwd,
    left_fwd,
    left_inv,
    right_inv,
    wanted,
    own_s,
    req,
    req_s,
    sendb,
    recvb,
    spec,
    part,
    ssend,
    srecv,
    bsend,
    brecv,
    load_sem,
    own_sem,
    local_sem,
    req_send,
    req_recv,
    fwd_send,
    fwd_recv,
    snap_send,
    snap_recv,
    back_send,
    back_recv,
):
    me = lax.axis_index("turb")
    sn = lax.axis_index("snap")
    side = vel.shape[-1]
    pairs, rows = pair_out.shape[:2]
    outs = 2 * turb_out.shape[0]
    chunks = pairs // BATCH
    cuts, tall = bsend.shape[1], bsend.shape[3]

    def ahead(k):
        return lax.rem(me + k, n)

    def behind(k):
        return lax.rem(me + n - k, n)

    def snap_at(j):
        return lax.rem(sn + j, ns)

    def others(step):
        def wrapped(i, carry):
            d = (i + 1) // 2
            step(n // 2 + d * (2 * (i % 2) - 1))
            return carry

        lax.fori_loop(0, n - 1, wrapped, 0)

    def loop(lo, hi, step):
        def wrapped(i, carry):
            step(i)
            return carry

        lax.fori_loop(lo, hi, wrapped, 0)

    loads = [
        pltpu.make_async_copy(a, b, load_sem.at[i])
        for i, (a, b) in enumerate(
            [
                (turb_rows_hbm, turb_rows),
                (wake_hbm, wake),
                (vel_hbm, vel),
                (right_fwd_hbm, right_fwd),
                (left_fwd_hbm, left_fwd),
                (left_inv_hbm, left_inv),
                (right_inv_hbm, right_inv),
            ]
        )
    ]
    for load in loads:
        load.start()
    barrier = pltpu.get_barrier_semaphore()
    loop(1, n, lambda k: pl.semaphore_signal(barrier, inc=1, device_id={"turb": ahead(k)}, device_id_type=MESH))
    loop(1, ns, lambda j: pl.semaphore_signal(barrier, inc=1, device_id={"snap": snap_at(j)}, device_id_type=MESH))
    for load in loads[:2]:
        load.wait()
    wanted[...] = tables(n, me, turb_out.shape[0], turb_rows, wake)[:, None, :]
    own = pltpu.make_async_copy(wanted, own_s, own_sem)
    own.start()
    pl.semaphore_wait(barrier, n + ns - 2)

    def req_copy(k):
        return pltpu.make_async_remote_copy(
            wanted.at[k], req.at[k], req_send.at[k], req_recv.at[k],
            device_id={"turb": behind(k)}, device_id_type=MESH,
        )

    def fwd_copy(k):
        return pltpu.make_async_remote_copy(
            sendb.at[k], recvb.at[k], fwd_send.at[k], fwd_recv.at[k],
            device_id={"turb": ahead(k)}, device_id_type=MESH,
        )

    def snap_copy(j, r):
        return pltpu.make_async_remote_copy(
            ssend.at[j, r], srecv.at[j, r], snap_send.at[j, r], snap_recv.at[j, r],
            device_id={"snap": snap_at(j)}, device_id_type=MESH,
        )

    def back_copy(k, r):
        return pltpu.make_async_remote_copy(
            bsend.at[k, r], brecv.at[k, r], back_send.at[k, r], back_recv.at[k, r],
            device_id={"turb": behind(k)}, device_id_type=MESH,
        )

    others(lambda k: req_copy(k).start())
    req[0] = wanted[0]
    loop(1, n, lambda k: req_copy(k).wait_recv())
    to_scalars = pltpu.make_async_copy(req, req_s, local_sem)
    to_scalars.start()
    to_scalars.wait()
    own.wait()
    for load in loads[2:]:
        load.wait()

    def send_planes(k):
        for c in range(CAP):
            sendb[k, c] = vel[req_s[k, 0, CAP + c]]
        fwd_copy(k).start()

    others(send_planes)
    for c in range(CAP):
        recvb[0, c] = vel[req_s[0, 0, CAP + c]]

    def forward(k):
        planes = recvb[k].reshape(CAP * side, side)
        half = dot(planes, right_fwd[...]).astype(jnp.bfloat16)
        top = jnp.concatenate([half[:side, :side], half[side:, :side]], axis=1)
        low = jnp.concatenate([half[:side, side:], half[side:, side:]], axis=1)
        both = dot(left_fwd[...], jnp.concatenate([top, low], axis=0)).astype(jnp.bfloat16)
        spec[k * CAP] = both[:, :side]
        spec[k * CAP + 1] = both[:, side:]

    forward(0)

    def arrive(k):
        fwd_copy(k).wait_recv()
        forward(k)

    others(arrive)

    def cross(p):
        up = spec[own_s[n, 0, p]].astype(jnp.float32)
        down = spec[own_s[n, 0, pairs + p]].astype(jnp.float32)
        ur, ui, dr, di = up[:side], up[side:], down[:side], down[side:]
        both = jnp.concatenate([ur * dr + ui * di, ur * di - ui * dr], axis=0)
        return (both * (1.0 / ns)).astype(jnp.bfloat16)

    def pair_chunk(c):
        for b in range(0, BATCH, 2):
            p = c * BATCH + b
            mixed = dot(left_inv[...], jnp.concatenate([cross(p), cross(p + 1)], axis=1)).astype(jnp.bfloat16)
            wide = jnp.concatenate(
                [
                    jnp.concatenate([mixed[:side, :side], mixed[side:, :side]], axis=1),
                    jnp.concatenate([mixed[:side, side:], mixed[side:, side:]], axis=1),
                ],
                axis=0,
            )
            out = dot(wide, right_inv[...])
            part[b] = out[:side]
            part[b + 1] = out[side:]
        for b in range(BATCH):
            p = c * BATCH + b
            pair_out[p] = part[b, pl.ds(pl.multiple_of(sn * rows, rows), rows)]

            def give(j):
                for r in range(cuts):
                    at = pl.multiple_of(snap_at(j) * rows, rows) + r * tall
                    ssend[j, r, p] = part[b, pl.ds(at, tall)].astype(jnp.bfloat16)

            loop(1, ns, give)

    loop(0, chunks, pair_chunk)
    for r in range(cuts):
        loop(1, ns, lambda j: snap_copy(j, r).start())

    for r in range(cuts):
        span = pl.ds(r * tall, tall)

        def collect(j):
            snap_copy(j, r).wait_recv()
            pair_out[:, span] = pair_out[:, span] + srecv[j, r].astype(jnp.float32)

        loop(1, ns, collect)

        def send_back(k):
            for c in range(CAP):
                bsend[k, r, c] = pair_out[own_s[k, 0, 2 * CAP + c], span].astype(jnp.bfloat16)
            back_copy(k, r).start()

        others(send_back)
        for c in range(CAP):
            brecv[0, r, c] = pair_out[own_s[0, 0, 2 * CAP + c], span].astype(jnp.bfloat16)

    turb_out[...] = jnp.zeros_like(turb_out)
    for r in range(cuts):
        span = pl.ds(r * tall, tall)

        def total(k):
            got = [brecv[k, r, c].astype(jnp.float32) for c in range(CAP)]
            codes = [req_s[k, 0, c] for c in range(CAP)]
            for o in range(outs):
                add = turb_out[o // 2, o % 2, span]
                for c in range(CAP):
                    add = add + got[c] * jnp.where(codes[c] == o, 1.0, 0.0)
                turb_out[o // 2, o % 2, span] = add

        total(0)

        def returned(k):
            back_copy(k, r).wait_recv()
            total(k)

        others(returned)

    def drain(k):
        req_copy(k).wait_send()
        fwd_copy(k).wait_send()
        for r in range(cuts):
            back_copy(k, r).wait_send()

    loop(1, n, drain)
    for r in range(cuts):
        loop(1, ns, lambda j: snap_copy(j, r).wait_send())


def write_out(pairs_in, turbs_in, pairs_out, turbs_out, sems):
    copies = [
        pltpu.make_async_copy(pairs_in, pairs_out, sems.at[0]),
        pltpu.make_async_copy(turbs_in, turbs_out, sems.at[1]),
    ]
    for copy in copies:
        copy.start()
    for copy in copies:
        copy.wait()


def body(velocity, turbine_rows, wake_pairs):
    n = lax.axis_size("turb")
    ns = lax.axis_size("snap")
    local_turb, local_snaps, side = velocity.shape[:3]
    assert local_snaps == 1
    pairs = wake_pairs.shape[0]
    total = turbine_rows.shape[0]
    slots = n * CAP
    rows = side // ns
    cuts = max(1, min(CUTS, rows // 16))
    assert local_turb & (local_turb - 1) == 0 and 2 * pairs <= 128
    wide_re, wide_im = basis_tables(side)
    re, im = wide_re.astype(ml_dtypes.bfloat16), wide_im.astype(ml_dtypes.bfloat16)
    right_fwd = np.concatenate([re, im], axis=1)
    left_fwd = np.block([[re, -im], [im, re]])
    left_inv = np.block([[re, im], [-im, re]])
    right_inv = np.concatenate([re, im], axis=0)
    basis = [jnp.asarray(a) for a in (right_fwd, left_fwd, left_inv, right_inv)]

    vmem = pl.BlockSpec(memory_space=pltpu.VMEM)
    hbm = pl.BlockSpec(memory_space=pltpu.HBM)
    bf16 = jnp.bfloat16
    sem = pltpu.SemaphoreType.DMA
    made = pl.pallas_call(
        functools.partial(kernel, n, ns),
        out_shape=(
            jax.ShapeDtypeStruct((pairs, rows, side), jnp.float32),
            jax.ShapeDtypeStruct((local_turb, 2, rows, side), jnp.float32),
        ),
        in_specs=[hbm] * 7,
        out_specs=(vmem, vmem),
        scratch_shapes=[
            pltpu.VMEM((1, total), jnp.int32),
            pltpu.VMEM((2, pairs), jnp.int32),
            pltpu.VMEM((local_turb, side, side), bf16),
            *[pltpu.VMEM(a.shape, bf16) for a in basis],
            pltpu.VMEM((n + 1, 1, 128), jnp.int32),
            pltpu.SMEM((n + 1, 1, 128), jnp.int32),
            pltpu.VMEM((n, 1, 128), jnp.int32),
            pltpu.SMEM((n, 1, 128), jnp.int32),
            pltpu.VMEM((n, CAP, side, side), bf16),
            pltpu.VMEM((n, CAP, side, side), bf16),
            pltpu.VMEM((slots, 2 * side, side), bf16),
            pltpu.VMEM((BATCH, side, side), jnp.float32),
            pltpu.VMEM((ns, cuts, pairs, rows // cuts, side), bf16),
            pltpu.VMEM((ns, cuts, pairs, rows // cuts, side), bf16),
            pltpu.VMEM((n, cuts, CAP, rows // cuts, side), bf16),
            pltpu.VMEM((n, cuts, CAP, rows // cuts, side), bf16),
            sem((7,)),
            sem,
            sem,
            sem((n,)),
            sem((n,)),
            sem((n,)),
            sem((n,)),
            sem((ns, cuts)),
            sem((ns, cuts)),
            sem((n, cuts)),
            sem((n, cuts)),
        ],
        compiler_params=pltpu.CompilerParams(
            collective_id=0, has_side_effects=True, vmem_limit_bytes=62 * 2**20
        ),
    )(velocity[:, 0], turbine_rows[None, :], wake_pairs.T, *basis)
    return pl.pallas_call(
        write_out,
        out_shape=tuple(jax.ShapeDtypeStruct(a.shape, a.dtype) for a in made),
        in_specs=[vmem] * 2,
        out_specs=(hbm, hbm),
        scratch_shapes=[sem((2,))],
    )(*made)


def solution(mesh):
    return jax.shard_map(
        body,
        mesh=mesh,
        in_specs=(P("turb", "snap", None, None), P(), P("turb", None)),
        out_specs=(P("turb", "snap", None), P("turb", None, "snap", None)),
        check_vma=False,
    )
```

```python
import functools

import jax
import jax.numpy as jnp
import ml_dtypes
import numpy as np
from jax import lax
from jax.experimental import pallas as pl
from jax.experimental.pallas import tpu as pltpu
from jax.sharding import PartitionSpec as P

MESH = pl.DeviceIdType.MESH
CAP = 2
BATCH = 16
CUTS = 2


def basis_tables(side):
    ramp = np.arange(side, dtype=np.int32)
    angles = (ramp[:, None] * ramp[None, :] % side) * (2.0 * np.pi / side)
    return (
        (np.cos(angles) / np.sqrt(side)).astype(np.float32),
        (-np.sin(angles) / np.sqrt(side)).astype(np.float32),
    )


def dot(a, b):
    return jnp.dot(a, b, preferred_element_type=jnp.float32)


def tables(n, me, local_turb, turb_rows, wake):
    pairs = wake.shape[1]
    count = 2 * pairs
    shift = local_turb.bit_length() - 1
    total = turb_rows.shape[1]
    first = lax.broadcasted_iota(jnp.int32, (pairs, pairs), 0)
    second = lax.broadcasted_iota(jnp.int32, (pairs, pairs), 1)
    ends = jnp.concatenate(
        [jnp.sum(jnp.where(first == second, wake[i : i + 1], 0), axis=1, keepdims=True) for i in range(2)], axis=0
    )
    lanes = lax.broadcasted_iota(jnp.int32, (count, total), 1)
    rows_col = jnp.sum(jnp.where(ends == lanes, turb_rows[...], 0), axis=1, keepdims=True)
    down = lax.broadcasted_iota(jnp.int32, (count, count), 0)
    over = lax.broadcasted_iota(jnp.int32, (count, count), 1)
    rows_row = jnp.sum(jnp.where(down == over, rows_col, 0), axis=0, keepdims=True)
    group_col = lax.shift_right_logical(rows_col, jnp.full_like(rows_col, shift))
    group_row = lax.shift_right_logical(rows_row, jnp.full_like(rows_row, shift))
    same = (group_col == group_row) & (down < over)
    rank = jnp.sum(jnp.where(same, 1, 0), axis=0, keepdims=True)
    back = me - group_row
    slot = jnp.where(back < 0, back + n, back) * CAP + rank
    end = lax.broadcasted_iota(jnp.int32, (1, count), 1)
    code = (rows_row - group_row * local_turb) * 2 + jnp.where(end >= pairs, 1, 0)
    pair = jnp.where(end >= pairs, end - pairs, end)
    place = lax.broadcasted_iota(jnp.int32, (n, count), 0)
    lane = lax.broadcasted_iota(jnp.int32, (n, 128), 1)
    table = jnp.zeros((n, 128), jnp.int32)
    for c in range(CAP):
        hit = slot == place * CAP + c
        codes = jnp.sum(jnp.where(hit, code + 1, 0), axis=1, keepdims=True) - 1
        owner = jnp.sum(jnp.where(hit, pair, 0), axis=1, keepdims=True)
        plane = lax.shift_right_logical(jnp.maximum(codes, 0), jnp.ones_like(codes))
        table = jnp.where(lane == c, codes, table)
        table = jnp.where(lane == CAP + c, plane, table)
        table = jnp.where(lane == 2 * CAP + c, owner, table)
    last = jnp.concatenate([jnp.minimum(slot, n * CAP - 1), jnp.zeros((1, 128 - count), jnp.int32)], axis=1)
    return jnp.concatenate([table, last], axis=0)


def kernel(
    n,
    ns,
    vel_hbm,
    turb_rows_hbm,
    wake_hbm,
    right_fwd_hbm,
    left_fwd_hbm,
    left_inv_hbm,
    right_inv_hbm,
    pair_out,
    turb_out,
    turb_rows,
    wake,
    vel,
    right_fwd,
    left_fwd,
    left_inv,
    right_inv,
    wanted,
    own_s,
    req,
    req_s,
    sendb,
    recvb,
    spec,
    part,
    ssend,
    srecv,
    bsend,
    brecv,
    load_sem,
    own_sem,
    local_sem,
    req_send,
    req_recv,
    fwd_send,
    fwd_recv,
    snap_send,
    snap_recv,
    back_send,
    back_recv,
):
    me = lax.axis_index("turb")
    sn = lax.axis_index("snap")
    side = vel.shape[-1]
    pairs, rows = pair_out.shape[:2]
    outs = 2 * turb_out.shape[0]
    chunks = pairs // BATCH
    cuts, tall = bsend.shape[1], bsend.shape[3]

    def ahead(k):
        return lax.rem(me + k, n)

    def behind(k):
        return lax.rem(me + n - k, n)

    def snap_at(j):
        return lax.rem(sn + j, ns)

    def others(step):
        def wrapped(i, carry):
            d = (i + 1) // 2
            step(n // 2 + d * (2 * (i % 2) - 1))
            return carry

        lax.fori_loop(0, n - 1, wrapped, 0)

    def loop(lo, hi, step):
        def wrapped(i, carry):
            step(i)
            return carry

        lax.fori_loop(lo, hi, wrapped, 0)

    loads = [
        pltpu.make_async_copy(a, b, load_sem.at[i])
        for i, (a, b) in enumerate(
            [
                (turb_rows_hbm, turb_rows),
                (wake_hbm, wake),
                (vel_hbm, vel),
                (right_fwd_hbm, right_fwd),
                (left_fwd_hbm, left_fwd),
                (left_inv_hbm, left_inv),
                (right_inv_hbm, right_inv),
            ]
        )
    ]
    for load in loads:
        load.start()
    barrier = pltpu.get_barrier_semaphore()
    loop(1, n, lambda k: pl.semaphore_signal(barrier, inc=1, device_id={"turb": ahead(k)}, device_id_type=MESH))
    loop(1, ns, lambda j: pl.semaphore_signal(barrier, inc=1, device_id={"snap": snap_at(j)}, device_id_type=MESH))
    for load in loads[:2]:
        load.wait()
    wanted[...] = tables(n, me, turb_out.shape[0], turb_rows, wake)[:, None, :]
    own = pltpu.make_async_copy(wanted, own_s, own_sem)
    own.start()
    pl.semaphore_wait(barrier, n + ns - 2)

    def req_copy(k):
        return pltpu.make_async_remote_copy(
            wanted.at[k], req.at[k], req_send.at[k], req_recv.at[k],
            device_id={"turb": behind(k)}, device_id_type=MESH,
        )

    def fwd_copy(k):
        return pltpu.make_async_remote_copy(
            sendb.at[k], recvb.at[k], fwd_send.at[k], fwd_recv.at[k],
            device_id={"turb": ahead(k)}, device_id_type=MESH,
        )

    def snap_copy(j, r):
        return pltpu.make_async_remote_copy(
            ssend.at[j, r], srecv.at[j, r], snap_send.at[j, r], snap_recv.at[j, r],
            device_id={"snap": snap_at(j)}, device_id_type=MESH,
        )

    def back_copy(k, r):
        return pltpu.make_async_remote_copy(
            bsend.at[k, r], brecv.at[k, r], back_send.at[k, r], back_recv.at[k, r],
            device_id={"turb": behind(k)}, device_id_type=MESH,
        )

    others(lambda k: req_copy(k).start())
    req[0] = wanted[0]
    loop(1, n, lambda k: req_copy(k).wait_recv())
    to_scalars = pltpu.make_async_copy(req, req_s, local_sem)
    to_scalars.start()
    to_scalars.wait()
    own.wait()
    for load in loads[2:]:
        load.wait()

    def send_planes(k):
        for c in range(CAP):
            sendb[k, c] = vel[req_s[k, 0, CAP + c]]
        fwd_copy(k).start()

    others(send_planes)
    for c in range(CAP):
        recvb[0, c] = vel[req_s[0, 0, CAP + c]]

    def forward(k):
        planes = recvb[k].reshape(CAP * side, side)
        half = dot(planes, right_fwd[...]).astype(jnp.bfloat16)
        top = jnp.concatenate([half[:side, :side], half[side:, :side]], axis=1)
        low = jnp.concatenate([half[:side, side:], half[side:, side:]], axis=1)
        both = dot(left_fwd[...], jnp.concatenate([top, low], axis=0)).astype(jnp.bfloat16)
        spec[k * CAP] = both[:, :side]
        spec[k * CAP + 1] = both[:, side:]

    forward(0)

    def arrive(k):
        fwd_copy(k).wait_recv()
        forward(k)

    others(arrive)

    def cross(p):
        up = spec[own_s[n, 0, p]].astype(jnp.float32)
        down = spec[own_s[n, 0, pairs + p]].astype(jnp.float32)
        ur, ui, dr, di = up[:side], up[side:], down[:side], down[side:]
        both = jnp.concatenate([ur * dr + ui * di, ur * di - ui * dr], axis=0)
        return (both * (1.0 / ns)).astype(jnp.bfloat16)

    def pair_chunk(c):
        for b in range(0, BATCH, 2):
            p = c * BATCH + b
            mixed = dot(left_inv[...], jnp.concatenate([cross(p), cross(p + 1)], axis=1)).astype(jnp.bfloat16)
            wide = jnp.concatenate(
                [
                    jnp.concatenate([mixed[:side, :side], mixed[side:, :side]], axis=1),
                    jnp.concatenate([mixed[:side, side:], mixed[side:, side:]], axis=1),
                ],
                axis=0,
            )
            out = dot(wide, right_inv[...])
            part[b] = out[:side]
            part[b + 1] = out[side:]
        for b in range(BATCH):
            p = c * BATCH + b
            pair_out[p] = part[b, pl.ds(pl.multiple_of(sn * rows, rows), rows)]

            def give(j):
                for r in range(cuts):
                    at = pl.multiple_of(snap_at(j) * rows, rows) + r * tall
                    ssend[j, r, p] = part[b, pl.ds(at, tall)].astype(jnp.bfloat16)

            loop(1, ns, give)

    loop(0, chunks, pair_chunk)
    for r in range(cuts):
        loop(1, ns, lambda j: snap_copy(j, r).start())

    for r in range(cuts):
        span = pl.ds(r * tall, tall)

        def collect(j):
            snap_copy(j, r).wait_recv()
            pair_out[:, span] = pair_out[:, span] + srecv[j, r].astype(jnp.float32)

        loop(1, ns, collect)

        def send_back(k):
            for c in range(CAP):
                bsend[k, r, c] = pair_out[own_s[k, 0, 2 * CAP + c], span].astype(jnp.bfloat16)
            back_copy(k, r).start()

        others(send_back)
        for c in range(CAP):
            brecv[0, r, c] = pair_out[own_s[0, 0, 2 * CAP + c], span].astype(jnp.bfloat16)

    turb_out[...] = jnp.zeros_like(turb_out)
    for r in range(cuts):
        span = pl.ds(r * tall, tall)

        def total(k):
            got = [brecv[k, r, c].astype(jnp.float32) for c in range(CAP)]
            codes = [req_s[k, 0, c] for c in range(CAP)]
            for o in range(outs):
                add = turb_out[o // 2, o % 2, span]
                for c in range(CAP):
                    add = add + got[c] * jnp.where(codes[c] == o, 1.0, 0.0)
                turb_out[o // 2, o % 2, span] = add

        total(0)

        def returned(k):
            back_copy(k, r).wait_recv()
            total(k)

        others(returned)

    def drain(k):
        req_copy(k).wait_send()
        fwd_copy(k).wait_send()
        for r in range(cuts):
            back_copy(k, r).wait_send()

    loop(1, n, drain)
    for r in range(cuts):
        loop(1, ns, lambda j: snap_copy(j, r).wait_send())


def write_out(pairs_in, turbs_in, pairs_out, turbs_out, sems):
    copies = [
        pltpu.make_async_copy(pairs_in, pairs_out, sems.at[0]),
        pltpu.make_async_copy(turbs_in, turbs_out, sems.at[1]),
    ]
    for copy in copies:
        copy.start()
    for copy in copies:
        copy.wait()


def body(velocity, turbine_rows, wake_pairs):
    n = lax.axis_size("turb")
    ns = lax.axis_size("snap")
    local_turb, local_snaps, side = velocity.shape[:3]
    assert local_snaps == 1
    pairs = wake_pairs.shape[0]
    total = turbine_rows.shape[0]
    slots = n * CAP
    rows = side // ns
    cuts = max(1, min(CUTS, rows // 16))
    assert local_turb & (local_turb - 1) == 0 and 2 * pairs <= 128
    wide_re, wide_im = basis_tables(side)
    re, im = wide_re.astype(ml_dtypes.bfloat16), wide_im.astype(ml_dtypes.bfloat16)
    right_fwd = np.concatenate([re, im], axis=1)
    left_fwd = np.block([[re, -im], [im, re]])
    left_inv = np.block([[re, im], [-im, re]])
    right_inv = np.concatenate([re, im], axis=0)
    basis = [jnp.asarray(a) for a in (right_fwd, left_fwd, left_inv, right_inv)]

    vmem = pl.BlockSpec(memory_space=pltpu.VMEM)
    hbm = pl.BlockSpec(memory_space=pltpu.HBM)
    bf16 = jnp.bfloat16
    sem = pltpu.SemaphoreType.DMA
    made = pl.pallas_call(
        functools.partial(kernel, n, ns),
        out_shape=(
            jax.ShapeDtypeStruct((pairs, rows, side), jnp.float32),
            jax.ShapeDtypeStruct((local_turb, 2, rows, side), jnp.float32),
        ),
        in_specs=[hbm] * 7,
        out_specs=(vmem, vmem),
        scratch_shapes=[
            pltpu.VMEM((1, total), jnp.int32),
            pltpu.VMEM((2, pairs), jnp.int32),
            pltpu.VMEM((local_turb, side, side), bf16),
            *[pltpu.VMEM(a.shape, bf16) for a in basis],
            pltpu.VMEM((n + 1, 1, 128), jnp.int32),
            pltpu.SMEM((n + 1, 1, 128), jnp.int32),
            pltpu.VMEM((n, 1, 128), jnp.int32),
            pltpu.SMEM((n, 1, 128), jnp.int32),
            pltpu.VMEM((n, CAP, side, side), bf16),
            pltpu.VMEM((n, CAP, side, side), bf16),
            pltpu.VMEM((slots, 2 * side, side), bf16),
            pltpu.VMEM((BATCH, side, side), jnp.float32),
            pltpu.VMEM((ns, cuts, pairs, rows // cuts, side), bf16),
            pltpu.VMEM((ns, cuts, pairs, rows // cuts, side), bf16),
            pltpu.VMEM((n, cuts, CAP, rows // cuts, side), bf16),
            pltpu.VMEM((n, cuts, CAP, rows // cuts, side), bf16),
            sem((7,)),
            sem,
            sem,
            sem((n,)),
            sem((n,)),
            sem((n,)),
            sem((n,)),
            sem((ns, cuts)),
            sem((ns, cuts)),
            sem((n, cuts)),
            sem((n, cuts)),
        ],
        compiler_params=pltpu.CompilerParams(
            collective_id=0, has_side_effects=True, vmem_limit_bytes=62 * 2**20
        ),
    )(velocity[:, 0], turbine_rows[None, :], wake_pairs.T, *basis)
    return pl.pallas_call(
        write_out,
        out_shape=tuple(jax.ShapeDtypeStruct(a.shape, a.dtype) for a in made),
        in_specs=[vmem] * 2,
        out_specs=(hbm, hbm),
        scratch_shapes=[sem((2,))],
    )(*made)


def solution(mesh):
    return jax.shard_map(
        body,
        mesh=mesh,
        in_specs=(P("turb", "snap", None, None), P(), P("turb", None)),
        out_specs=(P("turb", "snap", None), P("turb", None, "snap", None)),
        check_vma=False,
    )
```

```python
import functools

import jax
import jax.numpy as jnp
import ml_dtypes
import numpy as np
from jax import lax
from jax.experimental import pallas as pl
from jax.experimental.pallas import tpu as pltpu
from jax.sharding import PartitionSpec as P

MESH = pl.DeviceIdType.MESH
CAP = 2
BATCH = 16
CUTS = 4


def basis_tables(side):
    ramp = np.arange(side, dtype=np.int32)
    angles = (ramp[:, None] * ramp[None, :] % side) * (2.0 * np.pi / side)
    return (
        (np.cos(angles) / np.sqrt(side)).astype(np.float32),
        (-np.sin(angles) / np.sqrt(side)).astype(np.float32),
    )


def dot(a, b):
    return jnp.dot(a, b, preferred_element_type=jnp.float32)


def tables(n, me, local_turb, turb_rows, wake):
    pairs = wake.shape[1]
    count = 2 * pairs
    shift = local_turb.bit_length() - 1
    total = turb_rows.shape[1]
    first = lax.broadcasted_iota(jnp.int32, (pairs, pairs), 0)
    second = lax.broadcasted_iota(jnp.int32, (pairs, pairs), 1)
    ends = jnp.concatenate(
        [jnp.sum(jnp.where(first == second, wake[i : i + 1], 0), axis=1, keepdims=True) for i in range(2)], axis=0
    )
    lanes = lax.broadcasted_iota(jnp.int32, (count, total), 1)
    rows_col = jnp.sum(jnp.where(ends == lanes, turb_rows[...], 0), axis=1, keepdims=True)
    down = lax.broadcasted_iota(jnp.int32, (count, count), 0)
    over = lax.broadcasted_iota(jnp.int32, (count, count), 1)
    rows_row = jnp.sum(jnp.where(down == over, rows_col, 0), axis=0, keepdims=True)
    group_col = lax.shift_right_logical(rows_col, jnp.full_like(rows_col, shift))
    group_row = lax.shift_right_logical(rows_row, jnp.full_like(rows_row, shift))
    same = (group_col == group_row) & (down < over)
    rank = jnp.sum(jnp.where(same, 1, 0), axis=0, keepdims=True)
    back = me - group_row
    slot = jnp.where(back < 0, back + n, back) * CAP + rank
    end = lax.broadcasted_iota(jnp.int32, (1, count), 1)
    code = (rows_row - group_row * local_turb) * 2 + jnp.where(end >= pairs, 1, 0)
    pair = jnp.where(end >= pairs, end - pairs, end)
    place = lax.broadcasted_iota(jnp.int32, (n, count), 0)
    lane = lax.broadcasted_iota(jnp.int32, (n, 128), 1)
    table = jnp.zeros((n, 128), jnp.int32)
    for c in range(CAP):
        hit = slot == place * CAP + c
        codes = jnp.sum(jnp.where(hit, code + 1, 0), axis=1, keepdims=True) - 1
        owner = jnp.sum(jnp.where(hit, pair, 0), axis=1, keepdims=True)
        plane = lax.shift_right_logical(jnp.maximum(codes, 0), jnp.ones_like(codes))
        table = jnp.where(lane == c, codes, table)
        table = jnp.where(lane == CAP + c, plane, table)
        table = jnp.where(lane == 2 * CAP + c, owner, table)
    last = jnp.concatenate([jnp.minimum(slot, n * CAP - 1), jnp.zeros((1, 128 - count), jnp.int32)], axis=1)
    return jnp.concatenate([table, last], axis=0)


def kernel(
    n,
    ns,
    vel_hbm,
    turb_rows_hbm,
    wake_hbm,
    right_fwd_hbm,
    left_fwd_hbm,
    left_inv_hbm,
    right_inv_hbm,
    pair_out,
    turb_out,
    turb_rows,
    wake,
    vel,
    right_fwd,
    left_fwd,
    left_inv,
    right_inv,
    wanted,
    own_s,
    req,
    req_s,
    sendb,
    recvb,
    spec,
    part,
    ssend,
    srecv,
    bsend,
    brecv,
    load_sem,
    own_sem,
    local_sem,
    req_send,
    req_recv,
    fwd_send,
    fwd_recv,
    snap_send,
    snap_recv,
    back_send,
    back_recv,
):
    me = lax.axis_index("turb")
    sn = lax.axis_index("snap")
    side = vel.shape[-1]
    pairs, rows = pair_out.shape[:2]
    outs = 2 * turb_out.shape[0]
    chunks = pairs // BATCH
    cuts, tall = bsend.shape[1], bsend.shape[3]

    def ahead(k):
        return lax.rem(me + k, n)

    def behind(k):
        return lax.rem(me + n - k, n)

    def snap_at(j):
        return lax.rem(sn + j, ns)

    def others(step):
        def wrapped(i, carry):
            d = (i + 1) // 2
            step(n // 2 + d * (2 * (i % 2) - 1))
            return carry

        lax.fori_loop(0, n - 1, wrapped, 0)

    def loop(lo, hi, step):
        def wrapped(i, carry):
            step(i)
            return carry

        lax.fori_loop(lo, hi, wrapped, 0)

    loads = [
        pltpu.make_async_copy(a, b, load_sem.at[i])
        for i, (a, b) in enumerate(
            [
                (turb_rows_hbm, turb_rows),
                (wake_hbm, wake),
                (vel_hbm, vel),
                (right_fwd_hbm, right_fwd),
                (left_fwd_hbm, left_fwd),
                (left_inv_hbm, left_inv),
                (right_inv_hbm, right_inv),
            ]
        )
    ]
    for load in loads:
        load.start()
    barrier = pltpu.get_barrier_semaphore()
    loop(1, n, lambda k: pl.semaphore_signal(barrier, inc=1, device_id={"turb": ahead(k)}, device_id_type=MESH))
    loop(1, ns, lambda j: pl.semaphore_signal(barrier, inc=1, device_id={"snap": snap_at(j)}, device_id_type=MESH))
    for load in loads[:2]:
        load.wait()
    wanted[...] = tables(n, me, turb_out.shape[0], turb_rows, wake)[:, None, :]
    own = pltpu.make_async_copy(wanted, own_s, own_sem)
    own.start()
    pl.semaphore_wait(barrier, n + ns - 2)

    def req_copy(k):
        return pltpu.make_async_remote_copy(
            wanted.at[k], req.at[k], req_send.at[k], req_recv.at[k],
            device_id={"turb": behind(k)}, device_id_type=MESH,
        )

    def fwd_copy(k):
        return pltpu.make_async_remote_copy(
            sendb.at[k], recvb.at[k], fwd_send.at[k], fwd_recv.at[k],
            device_id={"turb": ahead(k)}, device_id_type=MESH,
        )

    def snap_copy(j, r):
        return pltpu.make_async_remote_copy(
            ssend.at[j, r], srecv.at[j, r], snap_send.at[j, r], snap_recv.at[j, r],
            device_id={"snap": snap_at(j)}, device_id_type=MESH,
        )

    def back_copy(k, r):
        return pltpu.make_async_remote_copy(
            bsend.at[k, r], brecv.at[k, r], back_send.at[k, r], back_recv.at[k, r],
            device_id={"turb": behind(k)}, device_id_type=MESH,
        )

    others(lambda k: req_copy(k).start())
    req[0] = wanted[0]
    loop(1, n, lambda k: req_copy(k).wait_recv())
    to_scalars = pltpu.make_async_copy(req, req_s, local_sem)
    to_scalars.start()
    to_scalars.wait()
    own.wait()
    for load in loads[2:]:
        load.wait()

    def send_planes(k):
        for c in range(CAP):
            sendb[k, c] = vel[req_s[k, 0, CAP + c]]
        fwd_copy(k).start()

    others(send_planes)
    for c in range(CAP):
        recvb[0, c] = vel[req_s[0, 0, CAP + c]]

    def forward(k):
        planes = recvb[k].reshape(CAP * side, side)
        half = dot(planes, right_fwd[...]).astype(jnp.bfloat16)
        top = jnp.concatenate([half[:side, :side], half[side:, :side]], axis=1)
        low = jnp.concatenate([half[:side, side:], half[side:, side:]], axis=1)
        both = dot(left_fwd[...], jnp.concatenate([top, low], axis=0)).astype(jnp.bfloat16)
        spec[k * CAP] = both[:, :side]
        spec[k * CAP + 1] = both[:, side:]

    forward(0)

    def arrive(k):
        fwd_copy(k).wait_recv()
        forward(k)

    others(arrive)

    def cross(p):
        up = spec[own_s[n, 0, p]].astype(jnp.float32)
        down = spec[own_s[n, 0, pairs + p]].astype(jnp.float32)
        ur, ui, dr, di = up[:side], up[side:], down[:side], down[side:]
        both = jnp.concatenate([ur * dr + ui * di, ur * di - ui * dr], axis=0)
        return (both * (1.0 / ns)).astype(jnp.bfloat16)

    def pair_chunk(c):
        for b in range(0, BATCH, 2):
            p = c * BATCH + b
            mixed = dot(left_inv[...], jnp.concatenate([cross(p), cross(p + 1)], axis=1)).astype(jnp.bfloat16)
            wide = jnp.concatenate(
                [
                    jnp.concatenate([mixed[:side, :side], mixed[side:, :side]], axis=1),
                    jnp.concatenate([mixed[:side, side:], mixed[side:, side:]], axis=1),
                ],
                axis=0,
            )
            out = dot(wide, right_inv[...])
            part[b] = out[:side]
            part[b + 1] = out[side:]
        for b in range(BATCH):
            p = c * BATCH + b
            pair_out[p] = part[b, pl.ds(pl.multiple_of(sn * rows, rows), rows)]

            def give(j):
                for r in range(cuts):
                    at = pl.multiple_of(snap_at(j) * rows, rows) + r * tall
                    ssend[j, r, p] = part[b, pl.ds(at, tall)].astype(jnp.bfloat16)

            loop(1, ns, give)

    loop(0, chunks, pair_chunk)
    for r in range(cuts):
        loop(1, ns, lambda j: snap_copy(j, r).start())

    for r in range(cuts):
        span = pl.ds(r * tall, tall)

        def collect(j):
            snap_copy(j, r).wait_recv()
            pair_out[:, span] = pair_out[:, span] + srecv[j, r].astype(jnp.float32)

        loop(1, ns, collect)

        def send_back(k):
            for c in range(CAP):
                bsend[k, r, c] = pair_out[own_s[k, 0, 2 * CAP + c], span].astype(jnp.bfloat16)
            back_copy(k, r).start()

        others(send_back)
        for c in range(CAP):
            brecv[0, r, c] = pair_out[own_s[0, 0, 2 * CAP + c], span].astype(jnp.bfloat16)

    turb_out[...] = jnp.zeros_like(turb_out)
    for r in range(cuts):
        span = pl.ds(r * tall, tall)

        def total(k):
            got = [brecv[k, r, c].astype(jnp.float32) for c in range(CAP)]
            codes = [req_s[k, 0, c] for c in range(CAP)]
            for o in range(outs):
                add = turb_out[o // 2, o % 2, span]
                for c in range(CAP):
                    add = add + got[c] * jnp.where(codes[c] == o, 1.0, 0.0)
                turb_out[o // 2, o % 2, span] = add

        total(0)

        def returned(k):
            back_copy(k, r).wait_recv()
            total(k)

        others(returned)

    def drain(k):
        req_copy(k).wait_send()
        fwd_copy(k).wait_send()
        for r in range(cuts):
            back_copy(k, r).wait_send()

    loop(1, n, drain)
    for r in range(cuts):
        loop(1, ns, lambda j: snap_copy(j, r).wait_send())


def write_out(pairs_in, turbs_in, pairs_out, turbs_out, sems):
    copies = [
        pltpu.make_async_copy(pairs_in, pairs_out, sems.at[0]),
        pltpu.make_async_copy(turbs_in, turbs_out, sems.at[1]),
    ]
    for copy in copies:
        copy.start()
    for copy in copies:
        copy.wait()


def body(velocity, turbine_rows, wake_pairs):
    n = lax.axis_size("turb")
    ns = lax.axis_size("snap")
    local_turb, local_snaps, side = velocity.shape[:3]
    assert local_snaps == 1
    pairs = wake_pairs.shape[0]
    total = turbine_rows.shape[0]
    slots = n * CAP
    rows = side // ns
    cuts = max(1, min(CUTS, rows // 16))
    assert local_turb & (local_turb - 1) == 0 and 2 * pairs <= 128
    wide_re, wide_im = basis_tables(side)
    re, im = wide_re.astype(ml_dtypes.bfloat16), wide_im.astype(ml_dtypes.bfloat16)
    right_fwd = np.concatenate([re, im], axis=1)
    left_fwd = np.block([[re, -im], [im, re]])
    left_inv = np.block([[re, im], [-im, re]])
    right_inv = np.concatenate([re, im], axis=0)
    basis = [jnp.asarray(a) for a in (right_fwd, left_fwd, left_inv, right_inv)]

    vmem = pl.BlockSpec(memory_space=pltpu.VMEM)
    hbm = pl.BlockSpec(memory_space=pltpu.HBM)
    bf16 = jnp.bfloat16
    sem = pltpu.SemaphoreType.DMA
    made = pl.pallas_call(
        functools.partial(kernel, n, ns),
        out_shape=(
            jax.ShapeDtypeStruct((pairs, rows, side), jnp.float32),
            jax.ShapeDtypeStruct((local_turb, 2, rows, side), jnp.float32),
        ),
        in_specs=[hbm] * 7,
        out_specs=(vmem, vmem),
        scratch_shapes=[
            pltpu.VMEM((1, total), jnp.int32),
            pltpu.VMEM((2, pairs), jnp.int32),
            pltpu.VMEM((local_turb, side, side), bf16),
            *[pltpu.VMEM(a.shape, bf16) for a in basis],
            pltpu.VMEM((n + 1, 1, 128), jnp.int32),
            pltpu.SMEM((n + 1, 1, 128), jnp.int32),
            pltpu.VMEM((n, 1, 128), jnp.int32),
            pltpu.SMEM((n, 1, 128), jnp.int32),
            pltpu.VMEM((n, CAP, side, side), bf16),
            pltpu.VMEM((n, CAP, side, side), bf16),
            pltpu.VMEM((slots, 2 * side, side), bf16),
            pltpu.VMEM((BATCH, side, side), jnp.float32),
            pltpu.VMEM((ns, cuts, pairs, rows // cuts, side), bf16),
            pltpu.VMEM((ns, cuts, pairs, rows // cuts, side), bf16),
            pltpu.VMEM((n, cuts, CAP, rows // cuts, side), bf16),
            pltpu.VMEM((n, cuts, CAP, rows // cuts, side), bf16),
            sem((7,)),
            sem,
            sem,
            sem((n,)),
            sem((n,)),
            sem((n,)),
            sem((n,)),
            sem((ns, cuts)),
            sem((ns, cuts)),
            sem((n, cuts)),
            sem((n, cuts)),
        ],
        compiler_params=pltpu.CompilerParams(
            collective_id=0, has_side_effects=True, vmem_limit_bytes=62 * 2**20
        ),
    )(velocity[:, 0], turbine_rows[None, :], wake_pairs.T, *basis)
    return pl.pallas_call(
        write_out,
        out_shape=tuple(jax.ShapeDtypeStruct(a.shape, a.dtype) for a in made),
        in_specs=[vmem] * 2,
        out_specs=(hbm, hbm),
        scratch_shapes=[sem((2,))],
    )(*made)


def solution(mesh):
    return jax.shard_map(
        body,
        mesh=mesh,
        in_specs=(P("turb", "snap", None, None), P(), P("turb", None)),
        out_specs=(P("turb", "snap", None), P("turb", None, "snap", None)),
        check_vma=False,
    )
```
